32 devices in a mesh: row: 8 (over z, core), col: 4 (over y, x).
Axes of the slice: x: 2, y: 2, z: 4, core: 2. Of those that a mesh axis runs over, the one named last changes fastest.
Arguments:
- raw_amps: float32 [2048, 3072], P('row', 'col'), may hold values from -24 to 24
- integrals: float32 [3072, 2048], P('row', 'col'), may hold values from -0.109375 to 0.109375
- occ_energy: float32 [256], replicated, may hold values from -2 to -0.5
- vir_energy: float32 [2048], replicated, may hold values from 0.5 to 3
- occ_pairs: int32 [2048, 2], P('row'), may hold values from 0 to 255
- vir_pairs: int32 [3072, 2], replicated, may hold values from 0 to 2047
- pair_order: int32 [3072], replicated, may hold values from 0 to 3071, each once
Outputs:
- residual: float32 [2048, 2048], P('row', 'col')
The draws below stay inside these ranges and needn't reach their ends.
Inputs may be any that keep to these rules, and one draw needn't show every extreme that they name: `pair_order`: each column index appears exactly once.
All inputs are finite; a program needn't handle non-finite values.
Results may differ from the reference program's by a relative error of at most 0.000068.
Values sent between devices are 32-bit elements; how exact they have to be, the bound alone decides.
No kernel may reach another device: no remote copies, remote signals or barrier semaphores. Data moves between devices by JAX's collectives and lax.ppermute only.
A program may use at most 64 MiB of HBM per device.

```python
import jax
import jax.numpy as jnp
from jax import lax

NO = 256
NV = 2048
K = 3072
P_SIZE = 2048
Q = 2048


def set_ends(array, stream_key, least, high):
    dims = array.shape
    index_at = [jax.random.randint(jax.random.fold_in(stream_key, axis), (), 0, dims[axis]) for axis in range(len(dims))]
    array = array.at[tuple(index_at)].set(least)
    longest = dims.index(max(dims))
    index_at[longest] = (index_at[longest] + 1) % dims[longest]
    return array.at[tuple(index_at)].set(high)


def steps_of(own_key, extent, shards, low, largest):
    factor_of = 1.0
    for dim, blocks in shards:
        heights = jax.random.uniform(jax.random.fold_in(jax.random.fold_in(own_key, 6), dim), (blocks,), jnp.float32, low / len(shards), largest / len(shards))
        factor_of = factor_of * jnp.repeat(jnp.exp(heights), extent[dim] // blocks).reshape((-1,) + (1,) * (len(extent) - 1 - dim))
    return factor_of


def noise(key, extent, spread, limit, split=(), kind=jnp.bfloat16):
    gain = steps_of(key, extent, split, -0.22, 0.18) if split else 1.0
    result = jax.random.normal(key, extent, jnp.float32) * spread * gain
    return jnp.minimum(jnp.maximum(result, -limit), limit).astype(kind)


def setup_inputs(seed: int = 0) -> dict:
    arg_keys = jax.random.split(jax.random.key(seed), 8)
    raw_amps = noise(arg_keys[0], (P_SIZE, K), 4.0, 24.0, ((0, 8), (1, 4)), jnp.float32)
    integrals = noise(arg_keys[1], (K, Q), K ** -0.5, 0.109375, ((0, 8), (1, 4)), jnp.float32)
    occ_energy = jnp.clip(jax.random.uniform(arg_keys[2], (NO,), jnp.float32, -2.0, -0.5), -2.0, -0.5)
    vir_energy = jnp.clip(jax.random.uniform(arg_keys[3], (NV,), jnp.float32, 0.5, 3.0), 0.5, 3.0)
    occ_pairs = set_ends(jax.random.randint(arg_keys[4], (P_SIZE, 2), 0, NO), jax.random.fold_in(arg_keys[4], 1), 0, NO - 1).astype(jnp.int32)
    vir_pairs = set_ends(jax.random.randint(arg_keys[5], (K, 2), 0, NV), jax.random.fold_in(arg_keys[5], 1), 0, NV - 1).astype(jnp.int32)
    pair_order = jax.random.permutation(arg_keys[6], K).astype(jnp.int32)
    return {"raw_amps": raw_amps, "integrals": integrals, "occ_energy": occ_energy, "vir_energy": vir_energy, "occ_pairs": occ_pairs, "vir_pairs": vir_pairs, "pair_order": pair_order}


def reference(raw_amps, integrals, occ_energy, vir_energy, occ_pairs, vir_pairs, pair_order):
    occ_sum = occ_energy[occ_pairs[:, 0]] + occ_energy[occ_pairs[:, 1]]
    vir_sum = vir_energy[vir_pairs[:, 0]] + vir_energy[vir_pairs[:, 1]]
    denom = vir_sum[None, :] - occ_sum[:, None]
    scaled = raw_amps / denom
    ordered = jnp.take(scaled, pair_order, axis=1)
    return jnp.dot(ordered, integrals, preferred_element_type=jnp.float32, precision=lax.Precision.HIGHEST)
```

```python
import functools

import jax
import jax.numpy as jnp
from jax import lax
from jax.experimental import pallas as pl
from jax.experimental.pallas import tpu as pltpu
from jax.sharding import PartitionSpec as P

LANES = 128
VMEM = pl.BlockSpec(memory_space=pltpu.VMEM)
SMEM = pl.BlockSpec(memory_space=pltpu.SMEM)
ANY = pl.BlockSpec(memory_space=pl.ANY)
PARAMS = pltpu.CompilerParams(vmem_limit_bytes=40 * 2**20)


def split(x):
    high = x.astype(jnp.bfloat16)
    return high, (x - high.astype(jnp.float32)).astype(jnp.bfloat16)


def look_up(energy, pairs, sums, column):
    tiles = energy.shape[0]
    for tile in range(tiles):
        column[pl.ds(tile * LANES, LANES), :] = jnp.broadcast_to(energy[tile : tile + 1, :], (LANES, LANES)).T
    width = 2 * LANES

    @pl.loop(0, pairs.shape[1] // width)
    def _(step):
        here = pl.ds(pl.multiple_of(step * width, width), width)
        first = jnp.broadcast_to(pairs[0:1, here], (8, width))
        second = jnp.broadcast_to(pairs[1:2, here], (8, width))
        sublane = lax.broadcasted_iota(jnp.int32, (8, width), 0)

        def add(group, total):
            value = column[pl.ds(pl.multiple_of(group * 8, 8), 8), :]
            value = jnp.concatenate([value, value], axis=1)
            index = sublane + group * 8
            return total + (jnp.where(index == first, value, 0.0) + jnp.where(index == second, value, 0.0))

        total = lax.fori_loop(0, tiles * (LANES // 8), add, jnp.zeros((8, width), jnp.float32), unroll=16)
        sums[0:1, here] = jnp.sum(total, axis=0, keepdims=True)


def energy_kernel(occ, vir, occ_pairs, vir_pairs, occ_sum, vir_sum, column):
    look_up(occ, occ_pairs, occ_sum, column)
    look_up(vir, vir_pairs, vir_sum, column)


def energy_sums(occ_energy, vir_energy, occ_pairs, vir_pairs):
    return pl.pallas_call(
        energy_kernel,
        name="energy_sums",
        out_shape=(
            jax.ShapeDtypeStruct((1, occ_pairs.shape[0]), jnp.float32),
            jax.ShapeDtypeStruct((1, vir_pairs.shape[0]), jnp.float32),
        ),
        scratch_shapes=[pltpu.VMEM((max(vir_energy.shape[0], occ_energy.shape[0]), LANES), jnp.float32)],
        compiler_params=PARAMS,
    )(occ_energy.reshape(-1, LANES), vir_energy.reshape(-1, LANES), occ_pairs.T, vir_pairs.T)


def divide_transposed(raw, occ_sum, vir_sum, vir_start, out, out_start):
    rows, width = raw.shape
    step = 2 * LANES if width % (2 * LANES) == 0 else LANES
    for start in range(0, width, step):
        vir = vir_sum[0:1, pl.ds(pl.multiple_of(vir_start + start, LANES), step)]
        vir = jnp.broadcast_to(vir, (LANES, step)).T
        vir = jnp.concatenate([vir] * (rows // LANES), axis=1)
        out[pl.ds(out_start + start, step), :] = raw[:, start : start + step].T / (vir - occ_sum[0:1, :])


def divide_kernel(count, starts, occ_sum, vir_sum, *refs):
    out = refs[count]
    width = refs[0].shape[1]
    for block in range(count):
        divide_transposed(refs[block], occ_sum, vir_sum, starts[block], out, block * width)


def divided(starts, occ_sum, vir_sum, *blocks):
    rows, width = blocks[0].shape
    return pl.pallas_call(
        functools.partial(divide_kernel, len(blocks)),
        name="divided",
        in_specs=[SMEM] + [VMEM] * (2 + len(blocks)),
        out_shape=jax.ShapeDtypeStruct((width * len(blocks), rows), jnp.float32),
        compiler_params=PARAMS,
    )(starts, occ_sum, vir_sum, *blocks)


def order_kernel(chunk, row_of, starts, bases, occ_sum, vir_sum, done, raw, high, low, held, rows, sem):
    size = done.shape[0]
    copy = pltpu.make_async_copy(done, held.at[pl.ds(0, size)], sem)
    copy.start()
    divide_transposed(raw, occ_sum, vir_sum, starts[starts.shape[0] - 1], held, size)
    copy.wait()
    per_block = high.shape[0] // bases.shape[0] // chunk

    @pl.loop(0, high.shape[0] // chunk)
    def _(step):
        base = bases[step // per_block] + (step % per_block) * chunk
        for row in range(chunk):
            rows[pl.ds(row, 1), :] = held[pl.ds(row_of[base + row], 1), :]
        here = pl.ds(pl.multiple_of(step * chunk, chunk), chunk)
        high[here, :], low[here, :] = split(rows[...])


def in_order(row_of, starts, bases, occ_sum, vir_sum, done, raw):
    pairs, rows = row_of.shape[0], raw.shape[0]
    chunk = LANES
    return pl.pallas_call(
        functools.partial(order_kernel, chunk),
        name="in_order",
        in_specs=[SMEM, SMEM, SMEM, VMEM, VMEM, ANY, VMEM],
        out_shape=(jax.ShapeDtypeStruct((pairs, rows), jnp.bfloat16),) * 2,
        scratch_shapes=[
            pltpu.VMEM((pairs, rows), jnp.float32),
            pltpu.VMEM((chunk, rows), jnp.float32),
            pltpu.SemaphoreType.DMA,
        ],
        compiler_params=PARAMS,
    )(row_of, starts, bases, occ_sum, vir_sum, done, raw)


def product(high, low, block):
    dot = functools.partial(
        lax.dot_general, dimension_numbers=(((0,), (0,)), ((), ())), preferred_element_type=jnp.float32
    )
    block_high, block_low = split(block)
    return dot(high, block_high) + (dot(high, block_low) + dot(low, block_high))


def product_kernel(count, has_total, high, low, *refs):
    blocks, refs = refs[:count], refs[count:]
    out, held, sems = refs[-3:]
    copies = [pltpu.make_async_copy(blocks[i], held.at[i], sems.at[i]) for i in range(count)]
    for copy in copies:
        copy.start()
    depth = held.shape[1]
    if has_total:
        out[...] = refs[0][...]
    else:
        out[...] = jnp.zeros_like(out)
    for i in range(count):
        copies[i].wait()
        here = pl.ds(i * depth, depth)
        out[...] += product(high[here, :], low[here, :], held[i])


def summed(high, low, part, blocks, total=None):
    depth, columns = blocks[0].shape
    count, rows = len(blocks), high.shape[1]
    ours = pl.BlockSpec((depth * count, rows), lambda i: (part, 0))
    whole = pl.BlockSpec((rows, columns), lambda i: (0, 0))
    return pl.pallas_call(
        functools.partial(product_kernel, count, total is not None),
        name="summed",
        grid=(1,),
        in_specs=[ours, ours] + [ANY] * count + ([whole] if total is not None else []),
        out_specs=whole,
        out_shape=jax.ShapeDtypeStruct((rows, columns), jnp.float32),
        scratch_shapes=[pltpu.VMEM((count, depth, columns), jnp.float32), pltpu.SemaphoreType.DMA((count,))],
        compiler_params=PARAMS,
    )(high, low, *blocks, *([total] if total is not None else []))


def four_chips_each(raw_amps, integrals, occ_energy, vir_energy, occ_pairs, vir_pairs, pair_order):
    row, col = lax.axis_index("row"), lax.axis_index("col")
    chip, core = row // 2, row % 2
    width, depth = raw_amps.shape[1], integrals.shape[0]

    def between_chips(block, pairs):
        return lax.ppermute(block, "row", [(2 * a + c, 2 * b + c) for a, b in pairs for c in range(2)])

    def other_core(block):
        return lax.ppermute(block, "row", [(i, i ^ 1) for i in range(8)])

    next_chip = between_chips(integrals, [(0, 1), (1, 0), (2, 3), (3, 2)])
    second_chip = between_chips(integrals, [(0, 2), (2, 0), (1, 3), (3, 1)])
    raw = [raw_amps] + [lax.ppermute(raw_amps, "col", [(i, i ^ m) for i in range(4)]) for m in (1, 2, 3)]
    far = between_chips(second_chip, [(1, 0), (2, 3)])
    middle = between_chips(integrals, [(1, 2), (2, 1)])
    third_chip = jnp.where((chip == 0) | (chip == 3), far, middle)

    occ_sum, vir_sum = energy_sums(occ_energy, vir_energy, occ_pairs, vir_pairs)
    starts = (col ^ jnp.arange(4, dtype=jnp.int32)) * width
    row_of = ((pair_order // width) ^ col) * width + pair_order % width
    bases = jnp.stack([((chip ^ m) * 2 + (core ^ s)) * depth for m in range(4) for s in range(2)])
    done = divided(starts[:3], occ_sum, vir_sum, *raw[:3])
    high, low = in_order(row_of, starts, bases, occ_sum, vir_sum, done, raw[3])

    blocks = []
    for block in (integrals, next_chip, second_chip):
        blocks += [block, other_core(block)]
    total = summed(high, low, 0, blocks)
    return summed(high, low, 3, [third_chip, other_core(third_chip)], total)


def any_mesh(raw_amps, integrals, occ_energy, vir_energy, occ_pairs, vir_pairs, pair_order):
    occ_sum, vir_sum = energy_sums(occ_energy, vir_energy, occ_pairs, vir_pairs)
    raw = lax.all_gather(raw_amps, "col", axis=1, tiled=True)
    half = raw.shape[1] // 2
    starts = jnp.arange(2, dtype=jnp.int32) * half
    done = divided(starts[:1], occ_sum, vir_sum, raw[:, :half])
    bases = jnp.zeros(1, jnp.int32)
    high, low = in_order(pair_order, starts, bases, occ_sum, vir_sum, done, raw[:, half:])
    return summed(high, low, 0, [lax.all_gather(integrals, "row", axis=0, tiled=True)])


def solution(mesh):
    placed = (P("row", "col"), P("row", "col"), P(), P(), P("row", None), P(), P())
    on_device = four_chips_each if (mesh.shape["row"], mesh.shape["col"]) == (8, 4) else any_mesh
    return jax.shard_map(
        on_device, mesh=mesh, in_specs=placed, out_specs=P("row", "col"), check_vma=False
    )
```

```python
import functools

import jax
import jax.numpy as jnp
from jax import lax
from jax.experimental import pallas as pl
from jax.experimental.pallas import tpu as pltpu
from jax.sharding import PartitionSpec as P

LANES = 128
VMEM = pl.BlockSpec(memory_space=pltpu.VMEM)
SMEM = pl.BlockSpec(memory_space=pltpu.SMEM)
ANY = pl.BlockSpec(memory_space=pl.ANY)
PARAMS = pltpu.CompilerParams(vmem_limit_bytes=40 * 2**20)


def split(x):
    high = x.astype(jnp.bfloat16)
    return high, (x - high.astype(jnp.float32)).astype(jnp.bfloat16)


def look_up(energy, pairs, sums, column):
    tiles = energy.shape[0]
    for tile in range(tiles):
        column[pl.ds(tile * LANES, LANES), :] = jnp.broadcast_to(energy[tile : tile + 1, :], (LANES, LANES)).T
    width = 2 * LANES

    @pl.loop(0, pairs.shape[1] // width)
    def _(step):
        here = pl.ds(pl.multiple_of(step * width, width), width)
        first = jnp.broadcast_to(pairs[0:1, here], (8, width))
        second = jnp.broadcast_to(pairs[1:2, here], (8, width))
        sublane = lax.broadcasted_iota(jnp.int32, (8, width), 0)

        def add(group, total):
            value = column[pl.ds(pl.multiple_of(group * 8, 8), 8), :]
            value = jnp.concatenate([value, value], axis=1)
            index = sublane + group * 8
            return total + (jnp.where(index == first, value, 0.0) + jnp.where(index == second, value, 0.0))

        total = lax.fori_loop(0, tiles * (LANES // 8), add, jnp.zeros((8, width), jnp.float32), unroll=16)
        sums[0:1, here] = jnp.sum(total, axis=0, keepdims=True)


def energy_kernel(occ, vir, occ_pairs, vir_pairs, occ_sum, vir_sum, column):
    look_up(occ, occ_pairs, occ_sum, column)
    look_up(vir, vir_pairs, vir_sum, column)


def energy_sums(occ_energy, vir_energy, occ_pairs, vir_pairs):
    return pl.pallas_call(
        energy_kernel,
        name="energy_sums",
        out_shape=(
            jax.ShapeDtypeStruct((1, occ_pairs.shape[0]), jnp.float32),
            jax.ShapeDtypeStruct((1, vir_pairs.shape[0]), jnp.float32),
        ),
        scratch_shapes=[pltpu.VMEM((max(vir_energy.shape[0], occ_energy.shape[0]), LANES), jnp.float32)],
        compiler_params=PARAMS,
    )(occ_energy.reshape(-1, LANES), vir_energy.reshape(-1, LANES), occ_pairs.T, vir_pairs.T)


def divide_transposed(raw, occ_sum, vir_sum, vir_start, out, out_start, out_column):
    rows, width = raw.shape
    step = 2 * LANES if width % (2 * LANES) == 0 else LANES
    columns = pl.ds(out_column, rows)
    for start in range(0, width, step):
        vir = vir_sum[0:1, pl.ds(pl.multiple_of(vir_start + start, LANES), step)]
        vir = jnp.broadcast_to(vir, (LANES, step)).T
        vir = jnp.concatenate([vir] * (rows // LANES), axis=1)
        out[pl.ds(out_start + start, step), columns] = raw[:, start : start + step].T / (vir - occ_sum[0:1, columns])


def divide_kernel(starts, occ_sum, vir_sum, *refs):
    blocks, (out, held, sems) = refs[:-3], refs[-3:]
    width = held.shape[2]
    copies = [pltpu.make_async_copy(block, held.at[i], sems.at[i]) for i, block in enumerate(blocks)]
    for copy in copies:
        copy.start()
    for i, copy in enumerate(copies):
        copy.wait()
        divide_transposed(held.at[i], occ_sum, vir_sum, starts[i], out, i * width, 0)


def divided(starts, occ_sum, vir_sum, *blocks):
    rows, width = blocks[0].shape
    count = len(blocks)
    return pl.pallas_call(
        divide_kernel,
        name="divided",
        in_specs=[SMEM, VMEM, VMEM] + [ANY] * count,
        out_shape=jax.ShapeDtypeStruct((width * count, rows), jnp.float32),
        scratch_shapes=[pltpu.VMEM((count, rows, width), jnp.float32), pltpu.SemaphoreType.DMA((count,))],
        compiler_params=PARAMS,
    )(starts, occ_sum, vir_sum, *blocks)


def order_kernel(chunk, row_of, starts, bases, occ_sum, vir_sum, done, *refs):
    parts, (high, low, held, raw, rows, sems, done_sem) = refs[:-7], refs[-7:]
    size, width = done.shape[0], raw.shape[1]
    copies, at = [], 0
    for i, part in enumerate(parts):
        copies.append(pltpu.make_async_copy(part, raw.at[pl.ds(at, part.shape[0])], sems.at[i]))
        copies[i].start()
        at += part.shape[0]
    done_copy = pltpu.make_async_copy(done, held.at[pl.ds(0, size)], done_sem)
    done_copy.start()
    at = 0
    for i, part in enumerate(parts):
        copies[i].wait()
        here = raw.at[pl.ds(at, part.shape[0])]
        divide_transposed(here, occ_sum, vir_sum, starts[starts.shape[0] - 1], held, size, at)
        at += part.shape[0]
    done_copy.wait()

    @pl.loop(0, high.shape[0] // chunk)
    def _(step):
        base = bases[step]
        for row in range(chunk):
            rows[pl.ds(row, 1), :] = held[pl.ds(row_of[base + row], 1), :]
        here = pl.ds(pl.multiple_of(step * chunk, chunk), chunk)
        high[here, :], low[here, :] = split(rows[...])


def in_order(row_of, starts, bases, occ_sum, vir_sum, done, *parts):
    pairs, rows = row_of.shape[0], done.shape[1]
    chunk = pairs // bases.shape[0]
    return pl.pallas_call(
        functools.partial(order_kernel, chunk),
        name="in_order",
        in_specs=[SMEM, SMEM, SMEM, VMEM, VMEM, ANY] + [ANY] * len(parts),
        out_shape=(jax.ShapeDtypeStruct((pairs, rows), jnp.bfloat16),) * 2,
        scratch_shapes=[
            pltpu.VMEM((pairs, rows), jnp.float32),
            pltpu.VMEM((rows, parts[0].shape[1]), jnp.float32),
            pltpu.VMEM((chunk, rows), jnp.float32),
            pltpu.SemaphoreType.DMA((len(parts),)),
            pltpu.SemaphoreType.DMA,
        ],
        compiler_params=PARAMS,
    )(row_of, starts, bases, occ_sum, vir_sum, done, *parts)


def product(high, low, block):
    dot = functools.partial(
        lax.dot_general, dimension_numbers=(((0,), (0,)), ((), ())), preferred_element_type=jnp.float32
    )
    block_high, block_low = split(block)
    return dot(high, block_high) + (dot(high, block_low) + dot(low, block_high))


def product_kernel(first, sizes, has_total, high, low, *refs):
    count = len(sizes)
    out, high_held, low_held, total_held, held, sems, more_sems = refs[-7:]
    starts = [sum(sizes[:i]) for i in range(count)]
    copies = [
        pltpu.make_async_copy(refs[i], held.at[pl.ds(starts[i], sizes[i])], sems.at[i]) for i in range(count)
    ]
    ours = pl.ds(first, sum(sizes))
    more = [
        pltpu.make_async_copy(high.at[ours], high_held, more_sems.at[0]),
        pltpu.make_async_copy(low.at[ours], low_held, more_sems.at[1]),
    ]
    if has_total:
        more.append(pltpu.make_async_copy(refs[count], total_held, more_sems.at[2]))
    for copy in more + copies:
        copy.start()
    for copy in more:
        copy.wait()
    for i in range(count):
        copies[i].wait()
        here = pl.ds(starts[i], sizes[i])
        term = product(high_held[here, :], low_held[here, :], held[here, :])
        if i == 0:
            out[...] = total_held[...] + term if has_total else term
        else:
            out[...] += term


def summed(high, low, first, blocks, total=None):
    sizes = [block.shape[0] for block in blocks]
    depth, columns, rows = sum(sizes), blocks[0].shape[1], high.shape[1]
    more = [total] if total is not None else []
    return pl.pallas_call(
        functools.partial(product_kernel, first, sizes, total is not None),
        name="summed",
        in_specs=[ANY, ANY] + [ANY] * len(blocks + more),
        out_specs=VMEM,
        out_shape=jax.ShapeDtypeStruct((rows, columns), jnp.float32),
        scratch_shapes=[
            pltpu.VMEM((depth, rows), jnp.bfloat16),
            pltpu.VMEM((depth, rows), jnp.bfloat16),
            pltpu.VMEM((rows, columns), jnp.float32),
            pltpu.VMEM((depth, columns), jnp.float32),
            pltpu.SemaphoreType.DMA((len(sizes),)),
            pltpu.SemaphoreType.DMA((3,)),
        ],
        compiler_params=PARAMS,
    )(high, low, *blocks, *more)


def four_chips_each(raw_amps, integrals, occ_energy, vir_energy, occ_pairs, vir_pairs, pair_order):
    row, col = lax.axis_index("row"), lax.axis_index("col")
    chip, core = row // 2, row % 2
    (rows, width), depth = raw_amps.shape, integrals.shape[0]

    def other_chip(block, mask):
        return lax.ppermute(block, "row", [(i, i ^ (2 * mask)) for i in range(8)])

    def other_core(block):
        return lax.ppermute(block, "row", [(i, i ^ 1) for i in range(8)])

    def across(block, mask):
        return lax.ppermute(block, "col", [(i, i ^ mask) for i in range(4)])

    next_chip, second_chip = other_chip(integrals, 1), other_chip(integrals, 2)
    raw_x, raw_y = across(raw_amps, 1), across(raw_amps, 2)

    occ_sum, vir_sum = energy_sums(occ_energy, vir_energy, occ_pairs, vir_pairs)
    starts = (col ^ jnp.arange(4, dtype=jnp.int32)) * width
    row_of = ((pair_order // width) ^ col) * width + pair_order % width
    runs = [(m, s, at) for m in range(4) for s in range(2) for at in range(0, depth, LANES)]
    bases = jnp.stack([((chip ^ m) * 2 + (core ^ s)) * depth + at for m, s, at in runs])

    raw_x, raw_y, vir_sum, bases, row_of = lax.optimization_barrier((raw_x, raw_y, vir_sum, bases, row_of))
    raw_d = [across(raw_x[: rows // 2], 2), across(raw_y[rows // 2 :], 1)]
    done = divided(starts[:3], occ_sum, vir_sum, raw_amps, raw_x, raw_y)

    second_chip, next_chip, done, *raw_d = lax.optimization_barrier((second_chip, next_chip, done, *raw_d))
    third_chip = other_chip(second_chip, 1)
    high, low = in_order(row_of, starts, bases, occ_sum, vir_sum, done, *raw_d)
    blocks = []
    for block in (integrals, next_chip, second_chip):
        blocks += [block, other_core(block)]
    total = summed(high, low, 0, blocks)
    third_chip, total = lax.optimization_barrier((third_chip, total))
    return summed(high, low, 6 * depth, [third_chip, other_core(third_chip)], total)


def any_mesh(raw_amps, integrals, occ_energy, vir_energy, occ_pairs, vir_pairs, pair_order):
    occ_sum, vir_sum = energy_sums(occ_energy, vir_energy, occ_pairs, vir_pairs)
    raw = lax.all_gather(raw_amps, "col", axis=1, tiled=True)
    half = raw.shape[1] // 2
    starts = jnp.arange(2, dtype=jnp.int32) * half
    done = divided(starts[:1], occ_sum, vir_sum, raw[:, :half])
    bases = jnp.arange(0, raw.shape[1], LANES, dtype=jnp.int32)
    high, low = in_order(pair_order, starts, bases, occ_sum, vir_sum, done, raw[:, half:])
    return summed(high, low, 0, [lax.all_gather(integrals, "row", axis=0, tiled=True)])


def solution(mesh):
    placed = (P("row", "col"), P("row", "col"), P(), P(), P("row", None), P(), P())
    on_device = four_chips_each if (mesh.shape["row"], mesh.shape["col"]) == (8, 4) else any_mesh
    return jax.shard_map(
        on_device, mesh=mesh, in_specs=placed, out_specs=P("row", "col"), check_vma=False
    )
```

```python
import functools

import jax
import jax.numpy as jnp
from jax import lax
from jax.experimental import pallas as pl
from jax.experimental.pallas import tpu as pltpu
from jax.sharding import PartitionSpec as P

LANES = 128
VMEM = pl.BlockSpec(memory_space=pltpu.VMEM)
SMEM = pl.BlockSpec(memory_space=pltpu.SMEM)
ANY = pl.BlockSpec(memory_space=pl.ANY)
PARAMS = pltpu.CompilerParams(vmem_limit_bytes=40 * 2**20)


def split(x):
    high = x.astype(jnp.bfloat16)
    return high, (x - high.astype(jnp.float32)).astype(jnp.bfloat16)


def look_up(energy, pairs, sums, column):
    tiles = energy.shape[0]
    for tile in range(tiles):
        column[pl.ds(tile * LANES, LANES), :] = jnp.broadcast_to(energy[tile : tile + 1, :], (LANES, LANES)).T
    width = 2 * LANES

    @pl.loop(0, pairs.shape[1] // width)
    def _(step):
        here = pl.ds(pl.multiple_of(step * width, width), width)
        first = jnp.broadcast_to(pairs[0:1, here], (8, width))
        second = jnp.broadcast_to(pairs[1:2, here], (8, width))
        sublane = lax.broadcasted_iota(jnp.int32, (8, width), 0)

        def add(group, total):
            value = column[pl.ds(pl.multiple_of(group * 8, 8), 8), :]
            value = jnp.concatenate([value, value], axis=1)
            index = sublane + group * 8
            return total + (jnp.where(index == first, value, 0.0) + jnp.where(index == second, value, 0.0))

        total = lax.fori_loop(0, tiles * (LANES // 8), add, jnp.zeros((8, width), jnp.float32), unroll=16)
        sums[0:1, here] = jnp.sum(total, axis=0, keepdims=True)


def energy_kernel(occ, vir, occ_pairs, vir_pairs, occ_sum, vir_sum, column):
    look_up(occ, occ_pairs, occ_sum, column)
    look_up(vir, vir_pairs, vir_sum, column)


def energy_sums(occ_energy, vir_energy, occ_pairs, vir_pairs):
    return pl.pallas_call(
        energy_kernel,
        name="energy_sums",
        out_shape=(
            jax.ShapeDtypeStruct((1, occ_pairs.shape[0]), jnp.float32),
            jax.ShapeDtypeStruct((1, vir_pairs.shape[0]), jnp.float32),
        ),
        scratch_shapes=[pltpu.VMEM((max(vir_energy.shape[0], occ_energy.shape[0]), LANES), jnp.float32)],
        compiler_params=PARAMS,
    )(occ_energy.reshape(-1, LANES), vir_energy.reshape(-1, LANES), occ_pairs.T, vir_pairs.T)


def divide_turned(raw, occ_sum, vir_sum, vir_start, held, at):
    rows, width = raw.shape
    tiles = rows // LANES
    step = 2 * LANES if width % (2 * LANES) == 0 else LANES
    for start in range(0, width, step):
        vir = vir_sum[0:1, pl.ds(pl.multiple_of(vir_start + start, LANES), step)]
        vir = jnp.broadcast_to(vir, (LANES, step)).T
        for tile in range(tiles):
            mine = pl.ds(tile * LANES, LANES)
            part = raw[mine, start : start + step].T / (vir - occ_sum[0:1, mine])
            held[pl.ds((at + start) * tiles + tile, step, stride=tiles), :] = part


def order_kernel(chunk, row_of, starts, bases, occ_sum, vir_sum, *refs):
    blocks, (high, low, raw, held, rows, sems) = refs[:-6], refs[-6:]
    width = raw.shape[2]
    tiles = high.shape[1] // LANES
    copies = [pltpu.make_async_copy(block, raw.at[i], sems.at[i]) for i, block in enumerate(blocks)]
    for copy in copies:
        copy.start()
    for i, copy in enumerate(copies):
        copy.wait()
        divide_turned(raw.at[i], occ_sum, vir_sum, starts[i], held, i * width)

    @pl.loop(0, high.shape[0] // chunk)
    def _(step):
        base = bases[step]
        for row in range(chunk):
            rows[pl.ds(row * tiles, tiles), :] = held[pl.ds(row_of[base + row], tiles), :]
        here = pl.ds(pl.multiple_of(step * chunk, chunk), chunk)
        for tile in range(tiles):
            mine = pl.ds(tile * LANES, LANES)
            high[here, mine], low[here, mine] = split(rows[pl.ds(tile, chunk, stride=tiles), :])


def ordered(place_of, starts, bases, occ_sum, vir_sum, *blocks):
    rows, width = blocks[0].shape
    pairs, count = place_of.shape[0], len(blocks)
    chunk, tiles = pairs // bases.shape[0], rows // LANES
    return pl.pallas_call(
        functools.partial(order_kernel, chunk),
        name="ordered",
        in_specs=[SMEM, SMEM, SMEM, VMEM, VMEM] + [ANY] * count,
        out_shape=(jax.ShapeDtypeStruct((pairs, rows), jnp.bfloat16),) * 2,
        scratch_shapes=[
            pltpu.VMEM((count, rows, width), jnp.float32),
            pltpu.VMEM((pairs * tiles, LANES), jnp.float32),
            pltpu.VMEM((chunk * tiles, LANES), jnp.float32),
            pltpu.SemaphoreType.DMA((count,)),
        ],
        compiler_params=PARAMS,
    )(place_of * tiles, starts, bases, occ_sum, vir_sum, *blocks)


def product(high, low, block):
    dot = functools.partial(
        lax.dot_general, dimension_numbers=(((0,), (0,)), ((), ())), preferred_element_type=jnp.float32
    )
    block_high, block_low = split(block)
    return dot(high, block_high) + (dot(high, block_low) + dot(low, block_high))


def product_kernel(first, sizes, has_total, high, low, *refs):
    count = len(sizes)
    out, high_held, low_held, total_held, held, sems, more_sems = refs[-7:]
    starts = [sum(sizes[:i]) for i in range(count)]
    copies = [
        pltpu.make_async_copy(refs[i], held.at[pl.ds(starts[i], sizes[i])], sems.at[i]) for i in range(count)
    ]
    ours = pl.ds(first, sum(sizes))
    more = [
        pltpu.make_async_copy(high.at[ours], high_held, more_sems.at[0]),
        pltpu.make_async_copy(low.at[ours], low_held, more_sems.at[1]),
    ]
    if has_total:
        more.append(pltpu.make_async_copy(refs[count], total_held, more_sems.at[2]))
    for copy in more + copies:
        copy.start()
    for copy in more:
        copy.wait()
    for i in range(count):
        copies[i].wait()
        here = pl.ds(starts[i], sizes[i])
        term = product(high_held[here, :], low_held[here, :], held[here, :])
        if i == 0:
            out[...] = total_held[...] + term if has_total else term
        else:
            out[...] += term


def summed(high, low, first, blocks, total=None):
    sizes = [block.shape[0] for block in blocks]
    depth, columns, rows = sum(sizes), blocks[0].shape[1], high.shape[1]
    more = [total] if total is not None else []
    return pl.pallas_call(
        functools.partial(product_kernel, first, sizes, total is not None),
        name="summed",
        in_specs=[ANY, ANY] + [ANY] * len(blocks + more),
        out_specs=VMEM,
        out_shape=jax.ShapeDtypeStruct((rows, columns), jnp.float32),
        scratch_shapes=[
            pltpu.VMEM((depth, rows), jnp.bfloat16),
            pltpu.VMEM((depth, rows), jnp.bfloat16),
            pltpu.VMEM((rows, columns), jnp.float32),
            pltpu.VMEM((depth, columns), jnp.float32),
            pltpu.SemaphoreType.DMA((len(sizes),)),
            pltpu.SemaphoreType.DMA((3,)),
        ],
        compiler_params=PARAMS,
    )(high, low, *blocks, *more)


def four_chips_each(raw_amps, integrals, occ_energy, vir_energy, occ_pairs, vir_pairs, pair_order):
    row, col = lax.axis_index("row"), lax.axis_index("col")
    chip, core = row // 2, row % 2
    width, depth = raw_amps.shape[1], integrals.shape[0]

    def other_chip(block, mask):
        return lax.ppermute(block, "row", [(i, i ^ (2 * mask)) for i in range(8)])

    def other_core(block):
        return lax.ppermute(block, "row", [(i, i ^ 1) for i in range(8)])

    def across(block, mask):
        return lax.ppermute(block, "col", [(i, i ^ mask) for i in range(4)])

    next_chip, second_chip = other_chip(integrals, 1), other_chip(integrals, 2)
    raw = [raw_amps] + [across(raw_amps, mask) for mask in (1, 2, 3)]
    crossed = other_core(integrals)
    crossed, vir_energy = lax.optimization_barrier((crossed, vir_energy))

    occ_sum, vir_sum = energy_sums(occ_energy, vir_energy, occ_pairs, vir_pairs)
    starts = (col ^ jnp.arange(4, dtype=jnp.int32)) * width
    place_of = ((pair_order // width) ^ col) * width + pair_order % width
    runs = [(m, s, at) for m, s in ((0, 0), (0, 1), (1, 0), (2, 0), (1, 1), (2, 1), (3, 0), (3, 1)) for at in range(0, depth, LANES)]
    bases = jnp.stack([((chip ^ m) * 2 + (core ^ s)) * depth + at for m, s, at in runs])

    second_chip, next_chip, vir_sum, bases, place_of = lax.optimization_barrier((second_chip, next_chip, vir_sum, bases, place_of))
    third_chip = other_chip(second_chip, 1)
    high, low = ordered(place_of, starts, bases, occ_sum, vir_sum, *raw)
    total = summed(high, low, 0, [integrals, crossed, next_chip, second_chip])
    third_chip, total = lax.optimization_barrier((third_chip, total))
    total = summed(high, low, 4 * depth, [other_core(next_chip), other_core(second_chip), third_chip], total)
    return summed(high, low, 7 * depth, [other_core(third_chip)], total)


def any_mesh(raw_amps, integrals, occ_energy, vir_energy, occ_pairs, vir_pairs, pair_order):
    occ_sum, vir_sum = energy_sums(occ_energy, vir_energy, occ_pairs, vir_pairs)
    raw = lax.all_gather(raw_amps, "col", axis=1, tiled=True)
    bases = jnp.arange(0, raw.shape[1], LANES, dtype=jnp.int32)
    high, low = ordered(pair_order, jnp.zeros(1, jnp.int32), bases, occ_sum, vir_sum, raw)
    return summed(high, low, 0, [lax.all_gather(integrals, "row", axis=0, tiled=True)])


def solution(mesh):
    placed = (P("row", "col"), P("row", "col"), P(), P(), P("row", None), P(), P())
    on_device = four_chips_each if (mesh.shape["row"], mesh.shape["col"]) == (8, 4) else any_mesh
    return jax.shard_map(
        on_device, mesh=mesh, in_specs=placed, out_specs=P("row", "col"), check_vma=False
    )
```

```python
import functools

import jax
import jax.numpy as jnp
from jax import lax
from jax.experimental import pallas as pl
from jax.experimental.pallas import tpu as pltpu
from jax.sharding import PartitionSpec as P

LANES = 128
RUN = 128
VMEM = pl.BlockSpec(memory_space=pltpu.VMEM)
SMEM = pl.BlockSpec(memory_space=pltpu.SMEM)
ANY = pl.BlockSpec(memory_space=pl.ANY)
PARAMS = pltpu.CompilerParams(vmem_limit_bytes=40 * 2**20)


def split(x):
    high = x.astype(jnp.bfloat16)
    return high, (x - high.astype(jnp.float32)).astype(jnp.bfloat16)


def look_up(energy, pairs, sums, column):
    tiles = energy.shape[0]
    for tile in range(tiles):
        column[pl.ds(tile * LANES, LANES), :] = jnp.broadcast_to(energy[tile : tile + 1, :], (LANES, LANES)).T
    width = 2 * LANES

    @pl.loop(0, pairs.shape[1] // width)
    def _(step):
        here = pl.ds(pl.multiple_of(step * width, width), width)
        first = jnp.broadcast_to(pairs[0:1, here], (8, width))
        second = jnp.broadcast_to(pairs[1:2, here], (8, width))
        sublane = lax.broadcasted_iota(jnp.int32, (8, width), 0)

        def add(group, total):
            value = column[pl.ds(pl.multiple_of(group * 8, 8), 8), :]
            value = jnp.concatenate([value, value], axis=1)
            index = sublane + group * 8
            return total + (jnp.where(index == first, value, 0.0) + jnp.where(index == second, value, 0.0))

        total = lax.fori_loop(0, tiles * (LANES // 8), add, jnp.zeros((8, width), jnp.float32), unroll=16)
        sums[0:1, here] = jnp.sum(total, axis=0, keepdims=True)


def energy_sums(energy, pairs, name, cost=None):
    return pl.pallas_call(
        look_up,
        name=name,
        out_shape=jax.ShapeDtypeStruct((1, pairs.shape[0]), jnp.float32),
        scratch_shapes=[pltpu.VMEM((energy.shape[0], LANES), jnp.float32)],
        compiler_params=PARAMS,
        cost_estimate=cost,
    )(energy.reshape(-1, LANES), pairs.T)


def divide_turned(raw, occ_sum, vir_sum, vir_start, held, at):
    rows, width = raw.shape
    tiles = rows // LANES
    step = 2 * LANES if width % (2 * LANES) == 0 else LANES
    for start in range(0, width, step):
        vir = vir_sum[0:1, pl.ds(pl.multiple_of(vir_start + start, LANES), step)]
        vir = jnp.broadcast_to(vir, (LANES, step)).T
        for tile in range(tiles):
            mine = pl.ds(tile * LANES, LANES)
            part = raw[mine, start : start + step].T / (vir - occ_sum[0:1, mine])
            held[pl.ds((at + start) * tiles + tile, step, stride=tiles), :] = part


def order_kernel(row_of, starts, bases, occ_sum, vir_sum, *refs):
    blocks, (high, low, held, rows) = refs[:-4], refs[-4:]
    width = blocks[0].shape[1]
    tiles = high.shape[0] // LANES
    for i, block in enumerate(blocks):
        divide_turned(block, occ_sum, vir_sum, starts[i], held, i * width)

    @pl.loop(0, high.shape[1] // RUN)
    def _(step):
        base = bases[step]
        for row in range(RUN):
            rows[pl.ds(row * tiles, tiles), :] = held[pl.ds(row_of[base + row], tiles), :]
        here = pl.ds(pl.multiple_of(step * RUN, RUN), RUN)
        for tile in range(tiles):
            mine = pl.ds(tile * LANES, LANES)
            high[mine, here], low[mine, here] = split(rows[pl.ds(tile, RUN, stride=tiles), :].T)


def ordered(place_of, starts, bases, occ_sum, vir_sum, *blocks):
    rows, pairs = blocks[0].shape[0], place_of.shape[0]
    tiles = rows // LANES
    return pl.pallas_call(
        order_kernel,
        name="ordered",
        in_specs=[SMEM, SMEM, SMEM] + [VMEM] * (2 + len(blocks)),
        out_shape=(jax.ShapeDtypeStruct((rows, pairs), jnp.bfloat16),) * 2,
        scratch_shapes=[
            pltpu.VMEM((pairs * tiles, LANES), jnp.float32),
            pltpu.VMEM((RUN * tiles, LANES), jnp.float32),
        ],
        compiler_params=PARAMS,
    )(place_of * tiles, starts, bases, occ_sum, vir_sum, *blocks)


def product(high, low, block):
    dot = functools.partial(jnp.dot, preferred_element_type=jnp.float32)
    block_high, block_low = split(block)
    return dot(high, block_high) + (dot(high, block_low) + dot(low, block_high))


def product_kernel(first, sizes, has_total, last, high, low, *refs):
    count = len(sizes)
    blocks, refs = refs[:count], refs[count:]
    total, refs = (refs[0], refs[1:]) if has_total else (None, refs)
    if last:
        out, result, sems = refs
    else:
        out = result = refs[0]
    parts = 2 if last else 1
    height = result.shape[0] // parts
    stores = []
    for i in range(count):
        here = pl.ds(first + sum(sizes[:i]), sizes[i])
        for part in range(parts):
            mine = pl.ds(part * height, height)
            term = product(high[mine, here], low[mine, here], blocks[i][...])
            if i == 0:
                result[mine, :] = total[mine, :] + term if has_total else term
            else:
                result[mine, :] += term
            if last and i == count - 1:
                stores.append(pltpu.make_async_copy(result.at[mine], out.at[mine], sems.at[part]))
                stores[part].start()
    for store in stores:
        store.wait()


def summed(high, low, first, blocks, total=None, last=False):
    sizes = [block.shape[0] for block in blocks]
    columns, rows = blocks[0].shape[1], high.shape[0]
    more = [total] if total is not None else []
    return pl.pallas_call(
        functools.partial(product_kernel, first, sizes, total is not None, last),
        name="summed",
        in_specs=[VMEM] * (2 + len(blocks) + len(more)),
        out_specs=ANY if last else VMEM,
        out_shape=jax.ShapeDtypeStruct((rows, columns), jnp.float32),
        scratch_shapes=[pltpu.VMEM((rows, columns), jnp.float32), pltpu.SemaphoreType.DMA((2,))] if last else [],
        compiler_params=PARAMS,
    )(high, low, *blocks, *more)


def four_chips_each(raw_amps, integrals, occ_energy, vir_energy, occ_pairs, vir_pairs, pair_order):
    row, col = lax.axis_index("row"), lax.axis_index("col")
    chip, core = row // 2, row % 2
    width, depth = raw_amps.shape[1], integrals.shape[0]

    def other_chip(block, mask):
        return lax.ppermute(block, "row", [(i, i ^ (2 * mask)) for i in range(8)])

    def other_core(block):
        return lax.ppermute(block, "row", [(i, i ^ 1) for i in range(8)])

    def across(block, mask):
        return lax.ppermute(block, "col", [(i, i ^ mask) for i in range(4)])

    next_chip, second_chip = other_chip(integrals, 1), other_chip(integrals, 2)
    raw = [across(raw_amps, mask) for mask in (1, 2, 3)]

    vir_sum = energy_sums(vir_energy, vir_pairs, "vir_sums")
    starts = (col ^ jnp.arange(4, dtype=jnp.int32)) * width
    place_of = ((pair_order // width) ^ col) * width + pair_order % width
    blocks = ((0, 0), (1, 0), (2, 0), (0, 1), (1, 1), (2, 1), (3, 0), (3, 1))
    runs = [(m, s, at) for m, s in blocks for at in range(0, depth, RUN)]
    bases = jnp.stack([((chip ^ m) * 2 + (core ^ s)) * depth + at for m, s, at in runs])

    second_chip, vir_sum, bases, place_of = lax.optimization_barrier((second_chip, vir_sum, bases, place_of))
    third_chip = other_chip(second_chip, 1)
    next_chip, occ_energy = lax.optimization_barrier((next_chip, occ_energy))
    occ_sum = energy_sums(occ_energy, occ_pairs, "occ_sums", None)
    *raw, occ_sum = lax.optimization_barrier((*raw, occ_sum))
    high, low = ordered(place_of, starts, bases, occ_sum, vir_sum, raw_amps, *raw)
    own = [integrals, next_chip, second_chip]
    total = summed(high, low, 0, own)
    third_chip, total = lax.optimization_barrier((third_chip, total))
    total = summed(high, low, 3 * depth, [other_core(block) for block in own] + [third_chip], total)
    return summed(high, low, 7 * depth, [other_core(third_chip)], total, last=True)


def any_mesh(raw_amps, integrals, occ_energy, vir_energy, occ_pairs, vir_pairs, pair_order):
    occ_sum = energy_sums(occ_energy, occ_pairs, "occ_sums")
    vir_sum = energy_sums(vir_energy, vir_pairs, "vir_sums")
    raw = lax.all_gather(raw_amps, "col", axis=1, tiled=True)
    bases = jnp.arange(0, raw.shape[1], RUN, dtype=jnp.int32)
    high, low = ordered(pair_order, jnp.zeros(1, jnp.int32), bases, occ_sum, vir_sum, raw)
    return summed(high, low, 0, [lax.all_gather(integrals, "row", axis=0, tiled=True)])


def solution(mesh):
    placed = (P("row", "col"), P("row", "col"), P(), P(), P("row", None), P(), P())
    on_device = four_chips_each if (mesh.shape["row"], mesh.shape["col"]) == (8, 4) else any_mesh
    return jax.shard_map(
        on_device, mesh=mesh, in_specs=placed, out_specs=P("row", "col"), check_vma=False
    )
```

```python
import functools

import jax
import jax.numpy as jnp
from jax import lax
from jax.experimental import pallas as pl
from jax.experimental.pallas import tpu as pltpu
from jax.sharding import PartitionSpec as P

LANES = 128
RUN = 128
VMEM = pl.BlockSpec(memory_space=pltpu.VMEM)
SMEM = pl.BlockSpec(memory_space=pltpu.SMEM)
ANY = pl.BlockSpec(memory_space=pl.ANY)
PARAMS = pltpu.CompilerParams(vmem_limit_bytes=40 * 2**20)


def split(x):
    high = x.astype(jnp.bfloat16)
    return high, (x - high.astype(jnp.float32)).astype(jnp.bfloat16)


def look_up(energy, pairs, sums, column):
    tiles = energy.shape[0]
    for tile in range(tiles):
        column[pl.ds(tile * LANES, LANES), :] = jnp.broadcast_to(energy[tile : tile + 1, :], (LANES, LANES)).T
    width = 2 * LANES

    @pl.loop(0, pairs.shape[1] // width)
    def _(step):
        here = pl.ds(pl.multiple_of(step * width, width), width)
        first = jnp.broadcast_to(pairs[0:1, here], (8, width))
        second = jnp.broadcast_to(pairs[1:2, here], (8, width))
        sublane = lax.broadcasted_iota(jnp.int32, (8, width), 0)

        def add(group, total):
            value = column[pl.ds(pl.multiple_of(group * 8, 8), 8), :]
            value = jnp.concatenate([value, value], axis=1)
            index = sublane + group * 8
            return total + (jnp.where(index == first, value, 0.0) + jnp.where(index == second, value, 0.0))

        total = lax.fori_loop(0, tiles * (LANES // 8), add, jnp.zeros((8, width), jnp.float32), unroll=16)
        sums[0:1, here] = jnp.sum(total, axis=0, keepdims=True)


def energy_sums(energy, pairs, name, cost=None):
    return pl.pallas_call(
        look_up,
        name=name,
        out_shape=jax.ShapeDtypeStruct((1, pairs.shape[0]), jnp.float32),
        scratch_shapes=[pltpu.VMEM((energy.shape[0], LANES), jnp.float32)],
        compiler_params=PARAMS,
        cost_estimate=cost,
    )(energy.reshape(-1, LANES), pairs.T)


def divide_turned(raw, occ_sum, vir_sum, vir_start, held, at):
    rows, width = raw.shape
    tiles = rows // LANES
    step = 2 * LANES if width % (2 * LANES) == 0 else LANES
    for start in range(0, width, step):
        vir = vir_sum[0:1, pl.ds(pl.multiple_of(vir_start + start, LANES), step)]
        vir = jnp.broadcast_to(vir, (LANES, step)).T
        for tile in range(tiles):
            mine = pl.ds(tile * LANES, LANES)
            part = raw[mine, start : start + step].T / (vir - occ_sum[0:1, mine])
            held[pl.ds((at + start) * tiles + tile, step, stride=tiles), :] = part


def order_kernel(row_of, starts, bases, occ_sum, vir_sum, *refs):
    blocks, (high, low, held, rows) = refs[:-4], refs[-4:]
    width = blocks[0].shape[1]
    tiles = high.shape[0] // LANES
    for i, block in enumerate(blocks):
        divide_turned(block, occ_sum, vir_sum, starts[i], held, i * width)

    @pl.loop(0, high.shape[1] // RUN)
    def _(step):
        base = bases[step]
        for row in range(RUN):
            rows[pl.ds(row * tiles, tiles), :] = held[pl.ds(row_of[base + row], tiles), :]
        here = pl.ds(pl.multiple_of(step * RUN, RUN), RUN)
        for tile in range(tiles):
            mine = pl.ds(tile * LANES, LANES)
            high[mine, here], low[mine, here] = split(rows[pl.ds(tile, RUN, stride=tiles), :].T)


def ordered(place_of, starts, bases, occ_sum, vir_sum, *blocks):
    rows, pairs = blocks[0].shape[0], place_of.shape[0]
    tiles = rows // LANES
    return pl.pallas_call(
        order_kernel,
        name="ordered",
        in_specs=[SMEM, SMEM, SMEM] + [VMEM] * (2 + len(blocks)),
        out_shape=(jax.ShapeDtypeStruct((rows, pairs), jnp.bfloat16),) * 2,
        scratch_shapes=[
            pltpu.VMEM((pairs * tiles + 8, LANES), jnp.float32),
            pltpu.VMEM((RUN * tiles + 8, LANES), jnp.float32),
        ],
        compiler_params=PARAMS,
    )(place_of * tiles, starts, bases, occ_sum, vir_sum, *blocks)


def product(high, low, block):
    block_high, block_low = split(block)
    return jnp.dot(
        jnp.concatenate([high, low, high], axis=1),
        jnp.concatenate([block_high, block_high, block_low], axis=0),
        preferred_element_type=jnp.float32,
    )


def product_kernel(first, sizes, has_total, last, high, low, *refs):
    count = len(sizes)
    blocks, refs = refs[:count], refs[count:]
    total, refs = (refs[0], refs[1:]) if has_total else (None, refs)
    if last:
        out, result, sems = refs
    else:
        out = result = refs[0]
    parts = 2 if last else 1
    height = result.shape[0] // parts
    stores = []
    for i in range(count):
        here = pl.ds(first + sum(sizes[:i]), sizes[i])
        for part in range(parts):
            mine = pl.ds(part * height, height)
            term = product(high[mine, here], low[mine, here], blocks[i][...])
            if i == 0:
                result[mine, :] = total[mine, :] + term if has_total else term
            else:
                result[mine, :] += term
            if last and i == count - 1:
                stores.append(pltpu.make_async_copy(result.at[mine], out.at[mine], sems.at[part]))
                stores[part].start()
    for store in stores:
        store.wait()


def summed(high, low, first, blocks, total=None, last=False):
    sizes = [block.shape[0] for block in blocks]
    columns, rows = blocks[0].shape[1], high.shape[0]
    more = [total] if total is not None else []
    return pl.pallas_call(
        functools.partial(product_kernel, first, sizes, total is not None, last),
        name="summed",
        in_specs=[VMEM] * (2 + len(blocks) + len(more)),
        out_specs=ANY if last else VMEM,
        out_shape=jax.ShapeDtypeStruct((rows, columns), jnp.float32),
        scratch_shapes=[pltpu.VMEM((rows, columns), jnp.float32), pltpu.SemaphoreType.DMA((2,))] if last else [],
        compiler_params=PARAMS,
    )(high, low, *blocks, *more)


def four_chips_each(raw_amps, integrals, occ_energy, vir_energy, occ_pairs, vir_pairs, pair_order):
    row, col = lax.axis_index("row"), lax.axis_index("col")
    chip, core = row // 2, row % 2
    width, depth = raw_amps.shape[1], integrals.shape[0]

    def between_chips(block, pairs):
        return lax.ppermute(block, "row", [(2 * a + c, 2 * b + c) for a, b in pairs for c in range(2)])

    def other_core(block):
        return lax.ppermute(block, "row", [(i, i ^ 1) for i in range(8)])

    def across(block, mask):
        return lax.ppermute(block, "col", [(i, i ^ mask) for i in range(4)])

    one = between_chips(integrals, [(0, 2), (3, 1), (1, 0), (2, 3)])
    two = between_chips(integrals, [(1, 3), (2, 0), (0, 1), (3, 2)])
    raw_x, raw_y = across(raw_amps, 1), across(raw_amps, 2)
    at_end = (chip == 0) | (chip == 3)

    vir_sum = energy_sums(vir_energy, vir_pairs, "vir_sums")
    starts = (col ^ jnp.arange(4, dtype=jnp.int32)) * width
    place_of = ((pair_order // width) ^ col) * width + pair_order % width
    blocks = ((0, 0, 0), (1, 2, 0), (2, 1, 0), (0, 0, 1), (1, 2, 1), (2, 1, 1), (3, 3, 0), (3, 3, 1))
    runs = [(jnp.where(at_end, end, inner), s, at) for end, inner, s in blocks for at in range(0, depth, RUN)]
    bases = jnp.stack([((chip ^ m) * 2 + (core ^ s)) * depth + at for m, s, at in runs])

    raw_d = across(raw_amps, 3)
    one, vir_sum, bases, place_of = lax.optimization_barrier((one, vir_sum, bases, place_of))
    far = between_chips(one, [(1, 0), (2, 3)])
    raw_x, own = lax.optimization_barrier((raw_x, integrals))
    middle = between_chips(own, [(1, 2), (2, 1)])
    third = jnp.where(at_end, far, middle)
    occ_sum = energy_sums(occ_energy, occ_pairs, "occ_sums")
    high, low = ordered(place_of, starts, bases, occ_sum, vir_sum, raw_amps, raw_x, raw_y, raw_d)
    total = summed(high, low, 0, [integrals, one, two])
    third, total = lax.optimization_barrier((third, total))
    crossed = [other_core(block) for block in (integrals, one, two)]
    total = summed(high, low, 3 * depth, crossed + [third], total)
    return summed(high, low, 7 * depth, [other_core(third)], total, last=True)


def any_mesh(raw_amps, integrals, occ_energy, vir_energy, occ_pairs, vir_pairs, pair_order):
    occ_sum = energy_sums(occ_energy, occ_pairs, "occ_sums")
    vir_sum = energy_sums(vir_energy, vir_pairs, "vir_sums")
    raw = lax.all_gather(raw_amps, "col", axis=1, tiled=True)
    bases = jnp.arange(0, raw.shape[1], RUN, dtype=jnp.int32)
    high, low = ordered(pair_order, jnp.zeros(1, jnp.int32), bases, occ_sum, vir_sum, raw)
    return summed(high, low, 0, [lax.all_gather(integrals, "row", axis=0, tiled=True)])


def solution(mesh):
    placed = (P("row", "col"), P("row", "col"), P(), P(), P("row", None), P(), P())
    on_device = four_chips_each if (mesh.shape["row"], mesh.shape["col"]) == (8, 4) else any_mesh
    return jax.shard_map(
        on_device, mesh=mesh, in_specs=placed, out_specs=P("row", "col"), check_vma=False
    )
```

```python
import functools

import jax
import jax.numpy as jnp
from jax import lax
from jax.experimental import pallas as pl
from jax.experimental.pallas import tpu as pltpu
from jax.sharding import PartitionSpec as P

LANES = 128
RUN = 128
VMEM = pl.BlockSpec(memory_space=pltpu.VMEM)
SMEM = pl.BlockSpec(memory_space=pltpu.SMEM)
ANY = pl.BlockSpec(memory_space=pl.ANY)
PARAMS = pltpu.CompilerParams(vmem_limit_bytes=40 * 2**20)


def split(x):
    high = x.astype(jnp.bfloat16)
    return high, (x - high.astype(jnp.float32)).astype(jnp.bfloat16)


def look_up(energy, pairs, sums, column):
    tiles = energy.shape[0]
    for tile in range(tiles):
        column[pl.ds(tile * LANES, LANES), :] = jnp.broadcast_to(energy[tile : tile + 1, :], (LANES, LANES)).T
    width = 2 * LANES

    @pl.loop(0, pairs.shape[1] // width)
    def _(step):
        here = pl.ds(pl.multiple_of(step * width, width), width)
        first = jnp.broadcast_to(pairs[0:1, here], (8, width))
        second = jnp.broadcast_to(pairs[1:2, here], (8, width))
        sublane = lax.broadcasted_iota(jnp.int32, (8, width), 0)

        def add(group, total):
            value = column[pl.ds(pl.multiple_of(group * 8, 8), 8), :]
            value = jnp.concatenate([value, value], axis=1)
            index = sublane + group * 8
            return total + (jnp.where(index == first, value, 0.0) + jnp.where(index == second, value, 0.0))

        total = lax.fori_loop(0, tiles * (LANES // 8), add, jnp.zeros((8, width), jnp.float32), unroll=16)
        sums[0:1, here] = jnp.sum(total, axis=0, keepdims=True)


def energy_sums(energy, pairs, name, cost=None):
    return pl.pallas_call(
        look_up,
        name=name,
        out_shape=jax.ShapeDtypeStruct((1, pairs.shape[0]), jnp.float32),
        scratch_shapes=[pltpu.VMEM((energy.shape[0], LANES), jnp.float32)],
        compiler_params=PARAMS,
        cost_estimate=cost,
    )(energy.reshape(-1, LANES), pairs.T)


def divide_turned(raw, occ_sum, vir_sum, vir_start, held, at):
    rows, width = raw.shape
    tiles = rows // LANES
    step = 2 * LANES if width % (2 * LANES) == 0 else LANES
    for start in range(0, width, step):
        vir = vir_sum[0:1, pl.ds(pl.multiple_of(vir_start + start, LANES), step)]
        vir = jnp.broadcast_to(vir, (LANES, step)).T
        for tile in range(tiles):
            mine = pl.ds(tile * LANES, LANES)
            part = raw[mine, start : start + step].T / (vir - occ_sum[0:1, mine])
            held[pl.ds((at + start) * tiles + tile, step, stride=tiles), :] = part


def order_kernel(row_of, starts, bases, occ_sum, vir_sum, *refs):
    blocks, (high, low, held, rows) = refs[:-4], refs[-4:]
    width = blocks[0].shape[1]
    tiles = high.shape[0] // LANES
    for i, block in enumerate(blocks):
        divide_turned(block, occ_sum, vir_sum, starts[i], held, i * width)

    @pl.loop(0, high.shape[1] // RUN)
    def _(step):
        base = bases[step]
        for row in range(RUN):
            rows[pl.ds(row * tiles, tiles), :] = held[pl.ds(row_of[base + row], tiles), :]
        here = pl.ds(pl.multiple_of(step * RUN, RUN), RUN)
        for tile in range(tiles):
            mine = pl.ds(tile * LANES, LANES)
            high[mine, here], low[mine, here] = split(rows[pl.ds(tile, RUN, stride=tiles), :].T)


def ordered(place_of, starts, bases, occ_sum, vir_sum, *blocks):
    rows, pairs = blocks[0].shape[0], place_of.shape[0]
    tiles = rows // LANES
    return pl.pallas_call(
        order_kernel,
        name="ordered",
        in_specs=[SMEM, SMEM, SMEM] + [VMEM] * (2 + len(blocks)),
        out_shape=(jax.ShapeDtypeStruct((rows, pairs), jnp.bfloat16),) * 2,
        scratch_shapes=[
            pltpu.VMEM((pairs * tiles + 8, LANES), jnp.float32),
            pltpu.VMEM((RUN * tiles + 8, LANES), jnp.float32),
        ],
        compiler_params=PARAMS,
    )(place_of * tiles, starts, bases, occ_sum, vir_sum, *blocks)


def product(high, low, block):
    block_high, block_low = split(block)
    return jnp.dot(
        jnp.concatenate([high, low, high], axis=1),
        jnp.concatenate([block_high, block_high, block_low], axis=0),
        preferred_element_type=jnp.float32,
    )


def product_kernel(first, sizes, has_total, last, high, low, *refs):
    count = len(sizes)
    blocks, refs = refs[:count], refs[count:]
    total, refs = (refs[0], refs[1:]) if has_total else (None, refs)
    if last:
        out, result, sems = refs
    else:
        out = result = refs[0]
    parts = 2 if last else 1
    height = result.shape[0] // parts
    stores = []
    for i in range(count):
        here = pl.ds(first + sum(sizes[:i]), sizes[i])
        for part in range(parts):
            mine = pl.ds(part * height, height)
            term = product(high[mine, here], low[mine, here], blocks[i][...])
            if i == 0:
                result[mine, :] = total[mine, :] + term if has_total else term
            else:
                result[mine, :] += term
            if last and i == count - 1:
                stores.append(pltpu.make_async_copy(result.at[mine], out.at[mine], sems.at[part]))
                stores[part].start()
    for store in stores:
        store.wait()


def summed(high, low, first, blocks, total=None, last=False):
    sizes = [block.shape[0] for block in blocks]
    columns, rows = blocks[0].shape[1], high.shape[0]
    more = [total] if total is not None else []
    return pl.pallas_call(
        functools.partial(product_kernel, first, sizes, total is not None, last),
        name="summed",
        in_specs=[VMEM] * (2 + len(blocks) + len(more)),
        out_specs=ANY if last else VMEM,
        out_shape=jax.ShapeDtypeStruct((rows, columns), jnp.float32),
        scratch_shapes=[pltpu.VMEM((rows, columns), jnp.float32), pltpu.SemaphoreType.DMA((2,))] if last else [],
        compiler_params=PARAMS,
    )(high, low, *blocks, *more)


def four_chips_each(raw_amps, integrals, occ_energy, vir_energy, occ_pairs, vir_pairs, pair_order):
    row, col = lax.axis_index("row"), lax.axis_index("col")
    chip, core = row // 2, row % 2
    width, depth = raw_amps.shape[1], integrals.shape[0]

    def between_chips(block, pairs):
        return lax.ppermute(block, "row", [(2 * a + c, 2 * b + c) for a, b in pairs for c in range(2)])

    def other_core(block):
        return lax.ppermute(block, "row", [(i, i ^ 1) for i in range(8)])

    def across(block, mask):
        return lax.ppermute(block, "col", [(i, i ^ mask) for i in range(4)])

    one = between_chips(integrals, [(0, 2), (3, 1), (1, 0), (2, 3)])
    two = between_chips(integrals, [(1, 3), (2, 0), (0, 1), (3, 2)])
    raw_x, raw_y, raw_d = [across(raw_amps, mask) for mask in (1, 2, 3)]
    at_end = (chip == 0) | (chip == 3)
    cut = 256

    crossed_own, vir_energy = lax.optimization_barrier((other_core(integrals), vir_energy))
    vir_sum = energy_sums(vir_energy, vir_pairs, "vir_sums")
    starts = (col ^ jnp.arange(4, dtype=jnp.int32)) * width
    place_of = ((pair_order // width) ^ col) * width + pair_order % width
    whole, first, second = range(0, depth, RUN), range(0, cut, RUN), range(cut, depth, RUN)
    blocks = [(end, inner, s, whole) for s in range(2) for end, inner in ((0, 0), (1, 2), (2, 1))]
    blocks += [(3, 3, s, part) for part in (first, second) for s in range(2)]
    runs = [(jnp.where(at_end, end, inner), s, at) for end, inner, s, part in blocks for at in part]
    bases = jnp.stack([((chip ^ m) * 2 + (core ^ s)) * depth + at for m, s, at in runs])

    occ_sum = energy_sums(occ_energy, occ_pairs, "occ_sums")
    one, vir_sum, occ_sum, starts, bases, place_of, mine = lax.optimization_barrier(
        (one, vir_sum, occ_sum, starts, bases, place_of, integrals)
    )
    far_a = between_chips(one[:cut], [(1, 0), (2, 3)])
    raw_x, mine = lax.optimization_barrier((raw_x, mine))
    middle = between_chips(mine, [(1, 2), (2, 1)])
    far_b = between_chips(one[cut:], [(1, 0), (2, 3)])
    high, low = ordered(place_of, starts, bases, occ_sum, vir_sum, raw_amps, raw_x, raw_y, raw_d)
    total = summed(high, low, 0, [integrals, one, two, crossed_own])
    far_a, middle, total = lax.optimization_barrier((far_a, middle, total))
    third_a = jnp.where(at_end, far_a, middle[:cut])
    crossed_a = other_core(third_a)
    total = summed(high, low, 4 * depth, [other_core(one), other_core(two)], total)
    far_b, total = lax.optimization_barrier((far_b, total))
    third_b = jnp.where(at_end, far_b, middle[cut:])
    total = summed(high, low, 6 * depth, [third_a, crossed_a, third_b], total)
    return summed(high, low, 7 * depth + cut, [other_core(third_b)], total, last=True)


def any_mesh(raw_amps, integrals, occ_energy, vir_energy, occ_pairs, vir_pairs, pair_order):
    occ_sum = energy_sums(occ_energy, occ_pairs, "occ_sums")
    vir_sum = energy_sums(vir_energy, vir_pairs, "vir_sums")
    raw = lax.all_gather(raw_amps, "col", axis=1, tiled=True)
    bases = jnp.arange(0, raw.shape[1], RUN, dtype=jnp.int32)
    high, low = ordered(pair_order, jnp.zeros(1, jnp.int32), bases, occ_sum, vir_sum, raw)
    return summed(high, low, 0, [lax.all_gather(integrals, "row", axis=0, tiled=True)])


def solution(mesh):
    placed = (P("row", "col"), P("row", "col"), P(), P(), P("row", None), P(), P())
    on_device = four_chips_each if (mesh.shape["row"], mesh.shape["col"]) == (8, 4) else any_mesh
    return jax.shard_map(
        on_device, mesh=mesh, in_specs=placed, out_specs=P("row", "col"), check_vma=False
    )
```

```python
import functools

import jax
import jax.numpy as jnp
from jax import lax
from jax.experimental import pallas as pl
from jax.experimental.pallas import tpu as pltpu
from jax.sharding import PartitionSpec as P

LANES = 128
RUN = 128
VMEM = pl.BlockSpec(memory_space=pltpu.VMEM)
SMEM = pl.BlockSpec(memory_space=pltpu.SMEM)
ANY = pl.BlockSpec(memory_space=pl.ANY)
PARAMS = pltpu.CompilerParams(vmem_limit_bytes=40 * 2**20)


def split(x):
    high = x.astype(jnp.bfloat16)
    return high, (x - high.astype(jnp.float32)).astype(jnp.bfloat16)


def look_up(energy, pairs, sums, column):
    tiles = energy.shape[0]
    for tile in range(tiles):
        column[pl.ds(tile * LANES, LANES), :] = jnp.broadcast_to(energy[tile : tile + 1, :], (LANES, LANES)).T
    width = 2 * LANES

    @pl.loop(0, pairs.shape[1] // width)
    def _(step):
        here = pl.ds(pl.multiple_of(step * width, width), width)
        first = jnp.broadcast_to(pairs[0:1, here], (8, width))
        second = jnp.broadcast_to(pairs[1:2, here], (8, width))
        sublane = lax.broadcasted_iota(jnp.int32, (8, width), 0)

        def add(group, total):
            value = column[pl.ds(pl.multiple_of(group * 8, 8), 8), :]
            value = jnp.concatenate([value, value], axis=1)
            index = sublane + group * 8
            return total + (jnp.where(index == first, value, 0.0) + jnp.where(index == second, value, 0.0))

        total = lax.fori_loop(0, tiles * (LANES // 8), add, jnp.zeros((8, width), jnp.float32), unroll=16)
        sums[0:1, here] = jnp.sum(total, axis=0, keepdims=True)


def energy_sums(energy, pairs, name, cost=None):
    return pl.pallas_call(
        look_up,
        name=name,
        out_shape=jax.ShapeDtypeStruct((1, pairs.shape[0]), jnp.float32),
        scratch_shapes=[pltpu.VMEM((energy.shape[0], LANES), jnp.float32)],
        compiler_params=PARAMS,
        cost_estimate=cost,
    )(energy.reshape(-1, LANES), pairs.T)


def divide_turned(raw, occ_sum, vir_sum, vir_start, held, at):
    rows, width = raw.shape
    tiles = rows // LANES
    step = 2 * LANES if width % (2 * LANES) == 0 else LANES
    for start in range(0, width, step):
        vir = vir_sum[0:1, pl.ds(pl.multiple_of(vir_start + start, LANES), step)]
        vir = jnp.broadcast_to(vir, (LANES, step)).T
        for tile in range(tiles):
            mine = pl.ds(tile * LANES, LANES)
            part = raw[mine, start : start + step].T / (vir - occ_sum[0:1, mine])
            held[pl.ds((at + start) * tiles + tile, step, stride=tiles), :] = part


def order_kernel(row_of, starts, bases, occ_sum, vir_sum, *refs):
    blocks, (high, low, held, rows) = refs[:-4], refs[-4:]
    width = blocks[0].shape[1]
    tiles = high.shape[0] // LANES
    for i, block in enumerate(blocks):
        divide_turned(block, occ_sum, vir_sum, starts[i], held, i * width)

    @pl.loop(0, high.shape[1] // RUN)
    def _(step):
        base = bases[step]
        for row in range(RUN):
            rows[pl.ds(row * tiles, tiles), :] = held[pl.ds(row_of[base + row], tiles), :]
        here = pl.ds(pl.multiple_of(step * RUN, RUN), RUN)
        for tile in range(tiles):
            mine = pl.ds(tile * LANES, LANES)
            high[mine, here], low[mine, here] = split(rows[pl.ds(tile, RUN, stride=tiles), :].T)


def ordered(place_of, starts, bases, occ_sum, vir_sum, *blocks):
    rows, pairs = blocks[0].shape[0], place_of.shape[0]
    tiles = rows // LANES
    return pl.pallas_call(
        order_kernel,
        name="ordered",
        in_specs=[SMEM, SMEM, SMEM] + [VMEM] * (2 + len(blocks)),
        out_shape=(jax.ShapeDtypeStruct((rows, pairs), jnp.bfloat16),) * 2,
        scratch_shapes=[
            pltpu.VMEM((pairs * tiles + 8, LANES), jnp.float32),
            pltpu.VMEM((RUN * tiles + 8, LANES), jnp.float32),
        ],
        compiler_params=PARAMS,
    )(place_of * tiles, starts, bases, occ_sum, vir_sum, *blocks)


def product(high, low, block):
    block_high, block_low = split(block)
    return jnp.dot(
        jnp.concatenate([high, low, high], axis=1),
        jnp.concatenate([block_high, block_high, block_low], axis=0),
        preferred_element_type=jnp.float32,
    )


def product_kernel(first, sizes, has_total, last, high, low, *refs):
    count = len(sizes)
    blocks, refs = refs[:count], refs[count:]
    total, refs = (refs[0], refs[1:]) if has_total else (None, refs)
    if last:
        out, result, sems = refs
    else:
        out = result = refs[0]
    parts = 2 if last else 1
    height = result.shape[0] // parts
    stores = []
    for i in range(count):
        here = pl.ds(first + sum(sizes[:i]), sizes[i])
        for part in range(parts):
            mine = pl.ds(part * height, height)
            term = product(high[mine, here], low[mine, here], blocks[i][...])
            if i == 0:
                result[mine, :] = total[mine, :] + term if has_total else term
            else:
                result[mine, :] += term
            if last and i == count - 1:
                stores.append(pltpu.make_async_copy(result.at[mine], out.at[mine], sems.at[part]))
                stores[part].start()
    for store in stores:
        store.wait()


def summed(high, low, first, blocks, total=None, last=False):
    sizes = [block.shape[0] for block in blocks]
    columns, rows = blocks[0].shape[1], high.shape[0]
    more = [total] if total is not None else []
    return pl.pallas_call(
        functools.partial(product_kernel, first, sizes, total is not None, last),
        name="summed",
        in_specs=[VMEM] * (2 + len(blocks) + len(more)),
        out_specs=ANY if last else VMEM,
        out_shape=jax.ShapeDtypeStruct((rows, columns), jnp.float32),
        scratch_shapes=[pltpu.VMEM((rows, columns), jnp.float32), pltpu.SemaphoreType.DMA((2,))] if last else [],
        compiler_params=PARAMS,
    )(high, low, *blocks, *more)


def four_chips_each(raw_amps, integrals, occ_energy, vir_energy, occ_pairs, vir_pairs, pair_order):
    row, col = lax.axis_index("row"), lax.axis_index("col")
    chip, core = row // 2, row % 2
    width, depth = raw_amps.shape[1], integrals.shape[0]

    def between_chips(block, pairs):
        return lax.ppermute(block, "row", [(2 * a + c, 2 * b + c) for a, b in pairs for c in range(2)])

    def other_core(block):
        return lax.ppermute(block, "row", [(i, i ^ 1) for i in range(8)])

    def across(block, mask):
        return lax.ppermute(block, "col", [(i, i ^ mask) for i in range(4)])

    one = between_chips(integrals, [(0, 2), (3, 1), (1, 0), (2, 3)])
    two = between_chips(integrals, [(1, 3), (2, 0), (0, 1), (3, 2)])
    raw_x, raw_y, raw_d = [across(raw_amps, mask) for mask in (1, 2, 3)]
    at_end = (chip == 0) | (chip == 3)
    cut = 256

    vir_sum = energy_sums(vir_energy, vir_pairs, "vir_sums")
    starts = (col ^ jnp.arange(4, dtype=jnp.int32)) * width
    place_of = ((pair_order // width) ^ col) * width + pair_order % width
    whole, first, second = range(0, depth, RUN), range(0, cut, RUN), range(cut, depth, RUN)
    blocks = [(end, inner, s, whole) for s in range(2) for end, inner in ((0, 0), (1, 2), (2, 1))]
    blocks += [(3, 3, s, part) for part in (first, second) for s in range(2)]
    runs = [(jnp.where(at_end, end, inner), s, at) for end, inner, s, part in blocks for at in part]
    bases = jnp.stack([((chip ^ m) * 2 + (core ^ s)) * depth + at for m, s, at in runs])

    occ_sum = energy_sums(occ_energy, occ_pairs, "occ_sums")
    one, vir_sum, occ_sum, starts, bases, place_of, mine = lax.optimization_barrier(
        (one, vir_sum, occ_sum, starts, bases, place_of, integrals)
    )
    far_a = between_chips(one[:cut], [(1, 0), (2, 3)])
    crossed = other_core(jnp.concatenate([mine, one]))
    raw_x, mine = lax.optimization_barrier((raw_x, mine))
    middle = between_chips(mine, [(1, 2), (2, 1)])
    far_b = between_chips(one[cut:], [(1, 0), (2, 3)])
    high, low = ordered(place_of, starts, bases, occ_sum, vir_sum, raw_amps, raw_x, raw_y, raw_d)
    total = summed(high, low, 0, [integrals, one, two])
    far_a, middle, total = lax.optimization_barrier((far_a, middle, total))
    third_a = jnp.where(at_end, far_a, middle[:cut])
    crossed_a = other_core(third_a)
    total = summed(high, low, 3 * depth, [crossed, other_core(two)], total)
    far_b, total = lax.optimization_barrier((far_b, total))
    third_b = jnp.where(at_end, far_b, middle[cut:])
    total = summed(high, low, 6 * depth, [third_a, crossed_a, third_b], total)
    return summed(high, low, 7 * depth + cut, [other_core(third_b)], total, last=True)


def any_mesh(raw_amps, integrals, occ_energy, vir_energy, occ_pairs, vir_pairs, pair_order):
    occ_sum = energy_sums(occ_energy, occ_pairs, "occ_sums")
    vir_sum = energy_sums(vir_energy, vir_pairs, "vir_sums")
    raw = lax.all_gather(raw_amps, "col", axis=1, tiled=True)
    bases = jnp.arange(0, raw.shape[1], RUN, dtype=jnp.int32)
    high, low = ordered(pair_order, jnp.zeros(1, jnp.int32), bases, occ_sum, vir_sum, raw)
    return summed(high, low, 0, [lax.all_gather(integrals, "row", axis=0, tiled=True)])


def solution(mesh):
    placed = (P("row", "col"), P("row", "col"), P(), P(), P("row", None), P(), P())
    on_device = four_chips_each if (mesh.shape["row"], mesh.shape["col"]) == (8, 4) else any_mesh
    return jax.shard_map(
        on_device, mesh=mesh, in_specs=placed, out_specs=P("row", "col"), check_vma=False
    )
```

```python
import functools

import jax
import jax.numpy as jnp
from jax import lax
from jax.experimental import pallas as pl
from jax.experimental.pallas import tpu as pltpu
from jax.sharding import PartitionSpec as P

LANES = 128
RUN = 128
VMEM = pl.BlockSpec(memory_space=pltpu.VMEM)
SMEM = pl.BlockSpec(memory_space=pltpu.SMEM)
ANY = pl.BlockSpec(memory_space=pl.ANY)
PARAMS = pltpu.CompilerParams(vmem_limit_bytes=40 * 2**20)


def split(x):
    high = x.astype(jnp.bfloat16)
    return high, (x - high.astype(jnp.float32)).astype(jnp.bfloat16)


def look_up(energy, pairs, sums, column):
    tiles = energy.shape[0]
    for tile in range(tiles):
        column[pl.ds(tile * LANES, LANES), :] = jnp.broadcast_to(energy[tile : tile + 1, :], (LANES, LANES)).T
    width = 2 * LANES

    @pl.loop(0, pairs.shape[1] // width)
    def _(step):
        here = pl.ds(pl.multiple_of(step * width, width), width)
        first = jnp.broadcast_to(pairs[0:1, here], (8, width))
        second = jnp.broadcast_to(pairs[1:2, here], (8, width))
        sublane = lax.broadcasted_iota(jnp.int32, (8, width), 0)

        def add(group, total):
            value = column[pl.ds(pl.multiple_of(group * 8, 8), 8), :]
            value = jnp.concatenate([value, value], axis=1)
            index = sublane + group * 8
            return total + (jnp.where(index == first, value, 0.0) + jnp.where(index == second, value, 0.0))

        total = lax.fori_loop(0, tiles * (LANES // 8), add, jnp.zeros((8, width), jnp.float32), unroll=16)
        sums[0:1, here] = jnp.sum(total, axis=0, keepdims=True)


def energy_sums(energy, pairs, name, cost=None):
    return pl.pallas_call(
        look_up,
        name=name,
        out_shape=jax.ShapeDtypeStruct((1, pairs.shape[0]), jnp.float32),
        scratch_shapes=[pltpu.VMEM((energy.shape[0], LANES), jnp.float32)],
        compiler_params=PARAMS,
        cost_estimate=cost,
    )(energy.reshape(-1, LANES), pairs.T)


def divide_turned(raw, occ_sum, vir_sum, vir_start, held, at):
    rows, width = raw.shape
    tiles = rows // LANES
    step = 2 * LANES if width % (2 * LANES) == 0 else LANES
    for start in range(0, width, step):
        vir = vir_sum[0:1, pl.ds(pl.multiple_of(vir_start + start, LANES), step)]
        vir = jnp.broadcast_to(vir, (LANES, step)).T
        for tile in range(tiles):
            mine = pl.ds(tile * LANES, LANES)
            part = raw[mine, start : start + step].T / (vir - occ_sum[0:1, mine])
            held[pl.ds((at + start) * tiles + tile, step, stride=tiles), :] = part


def order_kernel(row_of, starts, bases, occ_sum, vir_sum, *refs):
    blocks, (high, low, held, rows) = refs[:-4], refs[-4:]
    width = blocks[0].shape[1]
    tiles = high.shape[0] // LANES
    for i, block in enumerate(blocks):
        divide_turned(block, occ_sum, vir_sum, starts[i], held, i * width)

    @pl.loop(0, high.shape[1] // RUN)
    def _(step):
        base = bases[step]
        for row in range(RUN):
            rows[pl.ds(row * tiles, tiles), :] = held[pl.ds(row_of[base + row], tiles), :]
        here = pl.ds(pl.multiple_of(step * RUN, RUN), RUN)
        for tile in range(tiles):
            mine = pl.ds(tile * LANES, LANES)
            high[mine, here], low[mine, here] = split(rows[pl.ds(tile, RUN, stride=tiles), :].T)


def ordered(place_of, starts, bases, occ_sum, vir_sum, *blocks):
    rows, pairs = blocks[0].shape[0], place_of.shape[0]
    tiles = rows // LANES
    return pl.pallas_call(
        order_kernel,
        name="ordered",
        in_specs=[SMEM, SMEM, SMEM] + [VMEM] * (2 + len(blocks)),
        out_shape=(jax.ShapeDtypeStruct((rows, pairs), jnp.bfloat16),) * 2,
        scratch_shapes=[
            pltpu.VMEM((pairs * tiles + 8, LANES), jnp.float32),
            pltpu.VMEM((RUN * tiles + 8, LANES), jnp.float32),
        ],
        compiler_params=PARAMS,
    )(place_of * tiles, starts, bases, occ_sum, vir_sum, *blocks)


def product(high, low, block):
    block_high, block_low = split(block)
    return jnp.dot(
        jnp.concatenate([high, low, high], axis=1),
        jnp.concatenate([block_high, block_high, block_low], axis=0),
        preferred_element_type=jnp.float32,
    )


def product_kernel(first, sizes, has_total, last, high, low, *refs):
    count = len(sizes)
    blocks, refs = refs[:count], refs[count:]
    total, refs = (refs[0], refs[1:]) if has_total else (None, refs)
    if last:
        out, result, sems = refs
    else:
        out = result = refs[0]
    parts = 2 if last else 1
    height = result.shape[0] // parts
    stores = []
    for i in range(count):
        here = pl.ds(first + sum(sizes[:i]), sizes[i])
        for part in range(parts):
            mine = pl.ds(part * height, height)
            term = product(high[mine, here], low[mine, here], blocks[i][...])
            if i == 0:
                result[mine, :] = total[mine, :] + term if has_total else term
            else:
                result[mine, :] += term
            if last and i == count - 1:
                stores.append(pltpu.make_async_copy(result.at[mine], out.at[mine], sems.at[part]))
                stores[part].start()
    for store in stores:
        store.wait()


def summed(high, low, first, blocks, total=None, last=False):
    sizes = [block.shape[0] for block in blocks]
    columns, rows = blocks[0].shape[1], high.shape[0]
    more = [total] if total is not None else []
    return pl.pallas_call(
        functools.partial(product_kernel, first, sizes, total is not None, last),
        name="summed",
        in_specs=[VMEM] * (2 + len(blocks) + len(more)),
        out_specs=ANY if last else VMEM,
        out_shape=jax.ShapeDtypeStruct((rows, columns), jnp.float32),
        scratch_shapes=[pltpu.VMEM((rows, columns), jnp.float32), pltpu.SemaphoreType.DMA((2,))] if last else [],
        compiler_params=PARAMS,
    )(high, low, *blocks, *more)


def four_chips_each(raw_amps, integrals, occ_energy, vir_energy, occ_pairs, vir_pairs, pair_order):
    row, col = lax.axis_index("row"), lax.axis_index("col")
    chip, core = row // 2, row % 2
    width, depth = raw_amps.shape[1], integrals.shape[0]

    def between_chips(block, pairs):
        return lax.ppermute(block, "row", [(2 * a + c, 2 * b + c) for a, b in pairs for c in range(2)])

    def other_core(block):
        return lax.ppermute(block, "row", [(i, i ^ 1) for i in range(8)])

    def across(block, mask):
        return lax.ppermute(block, "col", [(i, i ^ mask) for i in range(4)])

    one = between_chips(integrals, [(0, 2), (3, 1), (1, 0), (2, 3)])
    two = between_chips(integrals, [(1, 3), (2, 0), (0, 1), (3, 2)])
    raw_x, raw_y, raw_d = [across(raw_amps, mask) for mask in (1, 2, 3)]
    at_end = (chip == 0) | (chip == 3)
    cut = 256

    vir_sum = energy_sums(vir_energy, vir_pairs, "vir_sums")
    starts = (col ^ jnp.arange(4, dtype=jnp.int32)) * width
    place_of = ((pair_order // width) ^ col) * width + pair_order % width
    whole, first, second = range(0, depth, RUN), range(0, cut, RUN), range(cut, depth, RUN)
    blocks = [(end, inner, s, whole) for s in range(2) for end, inner in ((0, 0), (1, 2), (2, 1))]
    blocks += [(3, 3, s, part) for part in (first, second) for s in range(2)]
    runs = [(jnp.where(at_end, end, inner), s, at) for end, inner, s, part in blocks for at in part]
    bases = jnp.stack([((chip ^ m) * 2 + (core ^ s)) * depth + at for m, s, at in runs])

    occ_sum = energy_sums(occ_energy, occ_pairs, "occ_sums")
    one, vir_sum, occ_sum, starts, bases, place_of, mine = lax.optimization_barrier(
        (one, vir_sum, occ_sum, starts, bases, place_of, integrals)
    )
    far_a = between_chips(one[:cut], [(1, 0), (2, 3)])
    crossed = other_core(jnp.concatenate([integrals, one]))
    raw_x, mine = lax.optimization_barrier((raw_x, mine))
    middle = between_chips(mine, [(1, 2), (2, 1)])
    far_b = between_chips(one[cut:], [(1, 0), (2, 3)])
    high, low = ordered(place_of, starts, bases, occ_sum, vir_sum, raw_amps, raw_x, raw_y, raw_d)
    total = summed(high, low, 0, [integrals, one, two])
    far_a, middle, total = lax.optimization_barrier((far_a, middle, total))
    third_a = jnp.where(at_end, far_a, middle[:cut])
    crossed_a = other_core(third_a)
    total = summed(high, low, 3 * depth, [crossed, other_core(two)], total)
    far_b, total = lax.optimization_barrier((far_b, total))
    third_b = jnp.where(at_end, far_b, middle[cut:])
    total = summed(high, low, 6 * depth, [third_a, crossed_a, third_b], total)
    return summed(high, low, 7 * depth + cut, [other_core(third_b)], total, last=True)


def any_mesh(raw_amps, integrals, occ_energy, vir_energy, occ_pairs, vir_pairs, pair_order):
    occ_sum = energy_sums(occ_energy, occ_pairs, "occ_sums")
    vir_sum = energy_sums(vir_energy, vir_pairs, "vir_sums")
    raw = lax.all_gather(raw_amps, "col", axis=1, tiled=True)
    bases = jnp.arange(0, raw.shape[1], RUN, dtype=jnp.int32)
    high, low = ordered(pair_order, jnp.zeros(1, jnp.int32), bases, occ_sum, vir_sum, raw)
    return summed(high, low, 0, [lax.all_gather(integrals, "row", axis=0, tiled=True)])


def solution(mesh):
    placed = (P("row", "col"), P("row", "col"), P(), P(), P("row", None), P(), P())
    on_device = four_chips_each if (mesh.shape["row"], mesh.shape["col"]) == (8, 4) else any_mesh
    return jax.shard_map(
        on_device, mesh=mesh, in_specs=placed, out_specs=P("row", "col"), check_vma=False
    )
```
